32 devices in a mesh: seq: 8 (over z, y), tower: 4 (over x, core).
Axes of the slice: x: 2, y: 2, z: 4, core: 2. Of those that a mesh axis runs over, the one named last changes fastest.
Arguments:
- inputs: bfloat16 [4, 1024, 4096], P('tower', 'seq'), may hold values from -21 to 21
- modality: int32 [4, 1024], P('tower', 'seq'), may hold values from 0 to 1, as said below
- segment: int32 [4, 1024], P('tower', 'seq'), may hold values from 0 to 7, never falling along the last dimension, each value on 1 to 512 neighbouring positions
- w_qkv: bfloat16 [2, 16, 4096, 384], P(None, 'seq', 'tower'), may hold values from -0.09375 to 0.09375
- w_out: bfloat16 [2, 16, 128, 4096], P(None, 'seq', None, 'tower'), may hold values from -0.5 to 0.5
Outputs:
- attended: bfloat16 [4, 1024, 4096], P('tower', 'seq')
The draws below stay inside these ranges and needn't reach their ends.
Inputs may be any that keep to these rules, and one draw needn't show every extreme that they name: `modality`: image positions come in contiguous runs. `segment`: within each packed sequence the document number never falls; every document holds 1 to 512 positions and one holds exactly 512.
All inputs are finite; a program needn't handle non-finite values.
Results may differ from the reference program's by a relative error of at most 0.012.
The reference program's roundings to bfloat16 on the way count: a program that leaves them out, or rounds other values in their place, can miss the bound.
Values may be sent and summed in bfloat16 or wider, within the bound.
A program may use at most 128 MiB of HBM per device.

```python
import math
import jax
import jax.numpy as jnp
import numpy as np
from jax import lax

D = 4096
H = 16
HD = 128
DOCS = 8
SEQS = 4
LEN = 1024
HEAD_DEV = 2


def draw_inputs(key, part):
    key = jax.random.fold_in(key, 11)
    value_key = jax.random.fold_in(key, 0)
    values = jax.random.truncated_normal(value_key, -6.0, 6.0, (SEQS, LEN, D), jnp.float32)
    return values.astype(jnp.bfloat16)


def draw_modality(key, part):
    key = jax.random.fold_in(key, 23)
    period_key, width_key, offset_key = jax.random.split(key, 3)
    period = jax.random.randint(period_key, (SEQS, 1), 4, 10)
    width = jax.random.randint(width_key, (SEQS, 1), 2, period)
    offset = jax.random.randint(offset_key, (SEQS, 1), 0, period)
    cell_rows = max(LEN // 16, 1)
    cells = jnp.arange(LEN, dtype=jnp.int32)[None, :] // cell_rows
    return ((cells + offset) % period < width).astype(jnp.int32)


def steps_of(own_key, dims, cuts, smallest, high):
    def one(position, shards_of):
        steps = jax.random.uniform(jax.random.fold_in(jax.random.fold_in(own_key, 6), position), (shards_of,), jnp.float32, smallest / len(cuts), high / len(cuts))
        return jnp.repeat(jnp.exp(steps), dims[position] // shards_of).reshape((-1,) + (1,) * (len(dims) - position - 1))

    factor_of = one(*cuts[0])
    for cut in cuts[1:]:
        factor_of = factor_of * one(*cut)
    return factor_of


def split_up(amount, total, reach, lean):
    loads = [(1 << 20) // math.isqrt(rank ** lean) + 1 for rank in range(2, amount + 1)]
    spare, given = total - reach - (amount - 1), [1] * (amount - 1)
    while spare > 0:
        movable = [i for i in range(amount - 1) if given[i] < reach]
        whole, remaining = sum([loads[i] for i in movable]), spare
        for i in movable:
            extra = min(reach - given[i], max(1, remaining * loads[i] // whole), spare)
            given[i] = given[i] + extra
            spare = spare - extra
    return np.array([reach] + given)


def uneven(stream_key, number_of, total, bound, skew):
    if number_of == 2:
        one = jax.random.randint(stream_key, (), max(1, total - bound), min(bound, total - 1) + 1)
        return jnp.stack([one, total - one])
    tallies = jnp.asarray(split_up(number_of, total, bound, skew), jnp.int32)
    twos = (number_of - 1) // 2
    donor, sink = tallies[1:1 + 2 * twos:2], tallies[2:2 + 2 * twos:2]
    room = jnp.minimum(donor - 1, bound - sink)
    moved = jax.random.randint(jax.random.fold_in(stream_key, 1), (twos,), 0, 1 << 20) % (room + 1)
    tallies = tallies.at[1:1 + 2 * twos:2].set(donor - moved).at[2:2 + 2 * twos:2].set(sink + moved)
    return tallies[jax.random.permutation(jax.random.fold_in(stream_key, 2), number_of)]


def scatter_about(stream_key, shape, deviation, most, cuts=(), held_as=jnp.bfloat16):
    gain = steps_of(stream_key, shape, cuts, -0.22, 0.18) if cuts else 1.0
    drawn = jax.random.normal(stream_key, shape, jnp.float32) * deviation * gain
    return jnp.minimum(jnp.maximum(drawn, -most), most).astype(held_as)


def setup_inputs(seed: int = 0) -> dict:
    splits = jax.random.split(jax.random.key(seed), 6)
    inputs = draw_inputs(jax.random.fold_in(splits[5], 71), 0)
    modality = draw_modality(jax.random.fold_in(splits[5], 71), 0)
    segment = jax.vmap(lambda own: jnp.searchsorted(jnp.cumsum(uneven(own, DOCS, LEN, LEN // 2, 2)), jnp.arange(LEN), side="right"))(jax.random.split(splits[2], SEQS)).reshape((SEQS, LEN)).astype(jnp.int32)
    w_qkv = scatter_about(splits[3], (2, H, D, 3 * HD), D ** -0.5, 0.09375, ((1, 8), (2, 4)))
    w_out = scatter_about(splits[4], (2, H, HD, D), HD ** -0.5, 0.5, ((1, 8), (3, 4)))
    return {"inputs": inputs, "modality": modality, "segment": segment, "w_qkv": w_qkv, "w_out": w_out}


def attend(queries, keys_all, values_all, doc_ids, score_scale):
    length = queries.shape[0]
    head_size = queries.shape[1]
    block_rows = min(512, length)
    positions = jnp.arange(length, dtype=jnp.int32)

    def one_block(block_idx):
        first_row = block_idx * block_rows
        q_block = lax.dynamic_slice_in_dim(queries, first_row, block_rows, 0)
        q_docs = lax.dynamic_slice_in_dim(doc_ids, first_row, block_rows, 0)
        q_pos = first_row + jnp.arange(block_rows, dtype=jnp.int32)
        scores = jnp.dot(q_block, keys_all.T, preferred_element_type=jnp.float32) * score_scale
        allowed = (q_docs[:, None] == doc_ids[None, :]) & (positions[None, :] <= q_pos[:, None])
        scores = jnp.where(allowed, scores, -jnp.inf)
        row_top = lax.optimization_barrier(jnp.max(scores, axis=1, keepdims=True))
        expon = jnp.exp(scores - row_top)
        probs = (expon / lax.optimization_barrier(jnp.sum(expon, axis=1, keepdims=True))).astype(jnp.bfloat16)
        return jnp.dot(probs, values_all, preferred_element_type=jnp.float32).astype(jnp.bfloat16)
    outputs = lax.map(one_block, jnp.arange(length // block_rows, dtype=jnp.int32))
    return outputs.reshape(length, head_size)

def reference(inputs, modality, segment, w_qkv, w_out):
    score_scale = 1.0 / math.sqrt(HD)
    wide_qkv = w_qkv.astype(jnp.float32)
    grouped_w = w_out.astype(jnp.float32).reshape(2, H // HEAD_DEV, HEAD_DEV, HD, D)
    highest = lax.Precision.HIGHEST

    def one_sequence(packed):
        tokens, modal_ids, doc_ids = packed
        wide_tokens = tokens.astype(jnp.float32)
        text_part = jnp.einsum('rd,hde->hre', wide_tokens, wide_qkv[0], precision=highest)
        image_part = jnp.einsum('rd,hde->hre', wide_tokens, wide_qkv[1], precision=highest)
        projected = jnp.where(modal_ids[None, :, None] == 1, image_part, text_part).astype(jnp.bfloat16)

        def one_head(qkv_head):
            return attend(qkv_head[:, :HD], qkv_head[:, HD:2 * HD], qkv_head[:, 2 * HD:], doc_ids, score_scale)
        head_out = lax.map(one_head, projected)
        grouped = head_out.reshape(H // HEAD_DEV, HEAD_DEV, LEN, HD)

        def add_group(running, group_idx):
            part_in = grouped[group_idx].astype(jnp.float32)
            text_out = jnp.einsum('hrc,hcd->rd', part_in, grouped_w[0, group_idx], precision=highest)
            image_out = jnp.einsum('hrc,hcd->rd', part_in, grouped_w[1, group_idx], precision=highest)
            chosen = jnp.where(modal_ids[:, None] == 1, image_out, text_out).astype(jnp.bfloat16)
            chosen = lax.optimization_barrier(chosen)
            return (running + chosen.astype(jnp.float32), None)
        total_sum, unused = lax.scan(add_group, jnp.zeros((LEN, D), jnp.float32), jnp.arange(H // HEAD_DEV, dtype=jnp.int32))
        return total_sum.astype(jnp.bfloat16)
    return lax.map(one_sequence, (inputs, modality, segment))
```

```python
import math

import jax
import jax.numpy as jnp
from jax import lax
from jax.experimental import pallas as pl
from jax.experimental.pallas import tpu as pltpu
from jax.sharding import PartitionSpec as P


def key_scores(q_block, keys_tile):
    return lax.dot_general(
        q_block, keys_tile, (((1,), (1,)), ((), ())), preferred_element_type=jnp.float32
    )


def dense_attend(queries, keys_all, values_all, doc_ids, score_scale):
    length = queries.shape[0]
    head_size = queries.shape[1]
    block_rows = min(512, length)
    positions = jnp.arange(length, dtype=jnp.int32)

    def one_block(block_idx):
        first_row = block_idx * block_rows
        q_block = lax.dynamic_slice_in_dim(queries, first_row, block_rows, 0)
        q_docs = lax.dynamic_slice_in_dim(doc_ids, first_row, block_rows, 0)
        q_pos = first_row + jnp.arange(block_rows, dtype=jnp.int32)
        scores = key_scores(q_block, keys_all) * score_scale
        allowed = (q_docs[:, None] == doc_ids[None, :]) & (positions[None, :] <= q_pos[:, None])
        scores = jnp.where(allowed, scores, -jnp.inf)
        row_top = jnp.max(scores, axis=1, keepdims=True)
        expon = jnp.exp(scores - row_top)
        probs = (expon / jnp.sum(expon, axis=1, keepdims=True)).astype(jnp.bfloat16)
        return jnp.dot(probs, values_all, preferred_element_type=jnp.float32).astype(jnp.bfloat16)

    outputs = lax.map(one_block, jnp.arange(length // block_rows, dtype=jnp.int32))
    return outputs.reshape(length, head_size)


def qkv_product(row_block, weight):
    return jnp.einsum("rd,hde->rhe", row_block, weight, preferred_element_type=jnp.float32)


def out_product(row_block, weight):
    return jnp.einsum("rhc,hcd->rd", row_block, weight, preferred_element_type=jnp.float32)


def local(inputs, modality, segment, w_qkv, w_out):
    tok_rows = inputs.shape[1]
    seq_devices = lax.axis_size("seq")
    length = tok_rows * seq_devices
    head_group = w_qkv.shape[1]
    head_size = w_out.shape[2]
    score_scale = 1.0 / math.sqrt(head_size)
    weights = lax.all_gather(w_qkv, "tower", axis=2, tiled=True)
    start_carry = (
        jnp.zeros((length, head_group, 3 * head_size), jnp.float32),
        jnp.zeros((length,), jnp.int32),
        jnp.zeros((length,), jnp.int32),
    )
    first_row = jnp.int32(0)
    row_piece = lax.all_gather(inputs, "seq", axis=1, tiled=True)
    modal_piece = lax.all_gather(modality, "seq", axis=1, tiled=True)
    doc_piece = lax.all_gather(segment, "seq", axis=1, tiled=True)
    text_part = qkv_product(row_piece[0], weights[0])
    image_part = qkv_product(row_piece[0], weights[1])
    selected = jnp.where(modal_piece[0][:, None, None] == 1, image_part, text_part)
    projected = selected
    modal_all = lax.dynamic_update_slice_in_dim(start_carry[1], modal_piece[0], first_row, 0)
    doc_all = lax.dynamic_update_slice_in_dim(start_carry[2], doc_piece[0], first_row, 0)
    projected = projected.astype(jnp.bfloat16)
    head_list = []
    for head_idx in range(head_group):
        queries = projected[:, head_idx, :head_size]
        keys_all = projected[:, head_idx, head_size : 2 * head_size]
        values_all = projected[:, head_idx, 2 * head_size :]
        head_list.append(dense_attend(queries, keys_all, values_all, doc_all, score_scale))
    head_out = jnp.stack(head_list, axis=0)
    columns = lax.all_gather(w_out, "tower", axis=3, tiled=True)
    out_rows = head_out
    out_rows = jnp.transpose(out_rows, (1, 0, 2))
    text_out = out_product(out_rows, columns[0])
    image_out = out_product(out_rows, columns[1])
    summed = lax.psum_scatter(
        jnp.where(modal_all[:, None] == 1, image_out, text_out).astype(jnp.bfloat16),
        "seq",
        scatter_dimension=0,
        tiled=True,
    )
    return summed[None]


MESH = pl.DeviceIdType.MESH


def coords():
    s, t = lax.axis_index("seq"), lax.axis_index("tower")
    return s, t, s // 2, s % 2, t // 2, t % 2


def enter(peers):
    barrier = pltpu.get_barrier_semaphore()
    for peer in peers:
        pl.semaphore_signal(barrier, inc=1, device_id=peer, device_id_type=MESH)
    pl.semaphore_wait(barrier, len(peers))


def remote(src, dst, send, recv, peer):
    return pltpu.make_async_remote_copy(
        src_ref=src, dst_ref=dst, send_sem=send, recv_sem=recv,
        device_id=peer, device_id_type=MESH,
    )


def gather_kernel(
    tok, meta, w, tok_all, meta_all, w_all,
    local_sem, up_send, dn_send, z_recv, y_send, y_recv,
    w_send, w_recv, m_send, m_recv, mt_send, mt_recv,
):
    s, t, z, y, x, c = coords()
    rows = tok.shape[0]
    depth = w.shape[2]
    x_peer = (s, (1 - x) * 2 + c)
    core_peer = (s, x * 2 + (1 - c))
    diagonal = (s, (1 - x) * 2 + (1 - c))
    y_peer = (z * 2 + (1 - y), t)
    seq_peers = [(lax.rem(s + k, 8), t) for k in range(1, 8)]
    enter(seq_peers + [x_peer, core_peer, diagonal])

    def tok_at(block):
        return tok_all.at[pl.ds(pl.multiple_of(block * rows, rows), rows)]

    def w_at(owner, m, h):
        return w_all.at[m, h, pl.ds(pl.multiple_of(owner * depth, depth), depth)]

    chunks = [(m, h) for m in range(w.shape[0]) for h in range(w.shape[1])]

    def up(o, src):
        return remote(src, tok_at(o * 2 + y), up_send.at[o], z_recv.at[o], (s + 2, t))

    def down(o, src):
        return remote(src, tok_at(o * 2 + y), dn_send.at[o], z_recv.at[o], (s - 2, t))

    def across(o, src):
        return remote(src, tok_at(o * 2 + y), y_send.at[o], y_recv.at[o], y_peer)

    def w_copy(kind, k, src, owner, peer):
        m, h = chunks[k]
        return remote(src, w_at(owner, m, h), w_send.at[kind, k], w_recv.at[kind, k], peer)

    @pl.when(z < 3)
    def _():
        up(z, tok).start()

    @pl.when(z > 0)
    def _():
        down(z, tok).start()

    across(z, tok).start()
    for k, (m, h) in enumerate(chunks):
        w_copy(0, k, w.at[m, h], t, x_peer).start()
    meta_copies = [
        remote(meta, meta_all.at[t, s], m_send.at[k], m_recv.at[k], peer)
        for k, peer in enumerate(seq_peers)
    ]
    for copy in meta_copies:
        copy.start()
    for k, (m, h) in enumerate(chunks):
        w_copy(1, k, w.at[m, h], t, core_peer).start()
    own = [
        pltpu.make_async_copy(tok, tok_at(s), local_sem.at[0]),
        pltpu.make_async_copy(meta, meta_all.at[t, s], local_sem.at[1]),
        pltpu.make_async_copy(
            w, w_all.at[:, :, pl.ds(pl.multiple_of(t * depth, depth), depth)], local_sem.at[2]
        ),
    ]
    for copy in own:
        copy.start()

    def pass_weights(k):
        m, h = chunks[k]
        w_copy(0, k, w.at[m, h], t, x_peer).wait_recv()
        w_copy(2, k, w_at(x_peer[1], m, h), x_peer[1], core_peer).start()

    n_chunks = len(chunks)
    for d in range(1, 4):
        if d - 1 < n_chunks:
            pass_weights(d - 1)
        low, high = z - d, z + d

        @pl.when(low >= 0)
        def _():
            up(low, tok_at(low * 2 + y)).wait_recv()

            @pl.when(z < 3)
            def _():
                up(low, tok_at(low * 2 + y)).start()

            across(low, tok_at(low * 2 + y)).start()

        @pl.when(high <= 3)
        def _():
            down(high, tok_at(high * 2 + y)).wait_recv()

            @pl.when(z > 0)
            def _():
                down(high, tok_at(high * 2 + y)).start()

            across(high, tok_at(high * 2 + y)).start()

    for k in range(3, n_chunks):
        pass_weights(k)
    for copy in own:
        copy.wait()
    for copy in meta_copies:
        copy.wait()
    tower_meta = [
        remote(meta_all.at[t], meta_all.at[t], mt_send.at[k], mt_recv.at[k], peer)
        for k, peer in enumerate((x_peer, core_peer, diagonal))
    ]
    for copy in tower_meta:
        copy.start()
    for o in range(4):
        across(o, tok).wait()

        @pl.when((z < 3) & (o <= z))
        def _():
            up(o, tok).wait_send()

        @pl.when((z > 0) & (o >= z))
        def _():
            down(o, tok).wait_send()

    for k, (m, h) in enumerate(chunks):
        w_copy(0, k, w.at[m, h], t, x_peer).wait_send()
        w_copy(1, k, w.at[m, h], t, core_peer).wait()
        w_copy(2, k, w.at[m, h], t, core_peer).wait()
    for copy in tower_meta:
        copy.wait()


def gather_all(tok, meta, w):
    dma = pltpu.SemaphoreType.DMA
    hbm = pl.BlockSpec(memory_space=pl.ANY)
    heads = w.shape[1]
    return pl.pallas_call(
        gather_kernel,
        out_shape=(
            jax.ShapeDtypeStruct((tok.shape[0] * 8, tok.shape[1]), tok.dtype),
            jax.ShapeDtypeStruct((4, 8) + meta.shape, meta.dtype),
            jax.ShapeDtypeStruct((2, heads, w.shape[2] * 4, w.shape[3]), w.dtype),
        ),
        in_specs=[hbm] * 3,
        out_specs=(hbm, hbm, hbm),
        scratch_shapes=[
            dma((3,)), dma((4,)), dma((4,)), dma((4,)), dma((4,)), dma((4,)),
            dma((3, 2 * heads)), dma((3, 2 * heads)), dma((7,)), dma((7,)), dma((3,)), dma((3,)),
        ],
        compiler_params=pltpu.CompilerParams(collective_id=0, has_side_effects=True),
        cost_estimate=pl.CostEstimate(flops=0, bytes_accessed=42 << 20, transcendentals=0),
    )(tok, meta, w)


def out_kernel(
    ho, mask, w, out, got, lhs, keep, sent, arrived, ready,
    z_send, z_recv, g_send, g_recv, y_send, y_recv, o_send, o_recv,
):
    s, t, z, y, x, c = coords()
    rows = ho.shape[0] // 4
    half = rows // 2
    width = ho.shape[1]
    cols = w.shape[2]
    order = [t, x * 2 + (1 - c), (1 - x) * 2 + c, (1 - x) * 2 + (1 - c)]
    x_peer, core_peer = (s, order[2]), (s, order[1])
    y_peer = (z * 2 + (1 - y), t)
    z_peers = [(lax.rem(s + 2 * k, 8), t) for k in range(1, 4)]
    enter(z_peers + [(s, o) for o in order[1:]] + [y_peer])

    def rows_of(block, n):
        return pl.ds(pl.multiple_of(block * n, n), n)

    z_copies = [
        remote(
            ho.at[rows_of(lax.rem(z + k, 4), rows)], got.at[t, z],
            z_send.at[k - 1], z_recv.at[k - 1], z_peers[k - 1],
        )
        for k in range(1, 4)
    ]
    for copy in z_copies:
        copy.start()
    got[t, z] = ho[rows_of(z, rows)]
    for copy in z_copies:
        copy.wait_recv()
    g_copies = [
        remote(got.at[t], got.at[t], g_send.at[0], g_recv.at[0], x_peer),
        remote(got.at[t], got.at[t], g_send.at[1], g_recv.at[1], core_peer),
        remote(got.at[order[2]], got.at[order[2]], g_send.at[2], g_recv.at[2], core_peer),
    ]
    g_copies[0].start()
    g_copies[1].start()

    def project(j):
        owner = order[j]
        for g in range(4):
            block = got[owner, g]
            m = mask[owner]
            for h in range(width // 128):
                part = block[:, h * 128:(h + 1) * 128]
                image = part * m
                lhs[g, :, h * 128:(h + 1) * 128] = part - image
                lhs[g, :, width + h * 128:width + (h + 1) * 128] = image

        @pl.loop(0, cols // 256)
        def _(tile):
            at = rows_of(tile, 256)
            for away in range(2):
                side = (1 - y) if away else y
                total = None
                for g in range(4):
                    part = jnp.dot(
                        lhs[g, rows_of(side, half), :], w[g, :, at],
                        preferred_element_type=jnp.float32,
                    ).astype(jnp.bfloat16).astype(jnp.float32)
                    total = part if total is None else total + part
                if away:
                    sent[j, :, at] = total.astype(jnp.bfloat16)
                else:
                    keep[j, :, at] = total

    y_copies = [
        remote(sent.at[j], arrived.at[j], y_send.at[j], y_recv.at[j], y_peer) for j in range(4)
    ]
    my_cols = rows_of(t, cols)
    o_copies = [
        remote(ready.at[j], out.at[:, my_cols], o_send.at[j - 1], o_recv.at[j - 1], (s, order[j]))
        for j in range(1, 4)
    ]

    def finish(j):
        y_copies[j].wait_recv()
        total = (keep[j] + arrived[j].astype(jnp.float32)).astype(jnp.bfloat16)
        if j == 0:
            out[:, my_cols] = total
        else:
            ready[j] = total
            o_copies[j - 1].start()

    project(0)
    y_copies[0].start()
    g_copies[1].wait_recv()
    project(1)
    y_copies[1].start()
    g_copies[0].wait_recv()
    g_copies[2].start()
    project(2)
    y_copies[2].start()
    finish(1)
    g_copies[2].wait_recv()
    project(3)
    y_copies[3].start()
    finish(0)
    finish(2)
    finish(3)
    for copy in z_copies + g_copies + y_copies:
        copy.wait_send()
    for copy in o_copies:
        copy.wait()


def out_project(ho, mask, w):
    dma = pltpu.SemaphoreType.DMA
    vmem = pl.BlockSpec(memory_space=pltpu.VMEM)
    rows, cols, width = ho.shape[0] // 4, w.shape[2], ho.shape[1]
    return pl.pallas_call(
        out_kernel,
        out_shape=jax.ShapeDtypeStruct((rows // 2, cols * 4), jnp.bfloat16),
        in_specs=[vmem] * 3,
        out_specs=vmem,
        scratch_shapes=[
            pltpu.VMEM((4, 4, rows, width), jnp.bfloat16),
            pltpu.VMEM((4, rows, 2 * width), jnp.bfloat16),
            pltpu.VMEM((4, rows // 2, cols), jnp.float32),
            pltpu.VMEM((4, rows // 2, cols), jnp.bfloat16),
            pltpu.VMEM((4, rows // 2, cols), jnp.bfloat16),
            pltpu.VMEM((4, rows // 2, cols), jnp.bfloat16),
            dma((3,)), dma((3,)), dma((3,)), dma((3,)), dma((4,)), dma((4,)), dma((3,)), dma((3,)),
        ],
        compiler_params=pltpu.CompilerParams(
            collective_id=1, has_side_effects=True, vmem_limit_bytes=40 << 20
        ),
        cost_estimate=pl.CostEstimate(
            flops=4 * 1024 * 1024 * 1024, bytes_accessed=8 << 20, transcendentals=0
        ),
    )(ho, mask, w)


def fast_local(inputs, modality, segment, w_qkv, w_out):
    heads, head_size = w_qkv.shape[1], w_out.shape[2]
    score_scale = 1.0 / math.sqrt(head_size)
    meta = jnp.concatenate([modality, segment, jnp.zeros((6, modality.shape[1]), jnp.int32)], axis=0)
    tok_all, meta_all, weights = gather_all(inputs[0], meta, w_qkv)
    s, t, z, y, x, c = coords()
    columns = lax.all_gather(
        w_out, "seq", axis_index_groups=[[0, 2, 4, 6], [1, 3, 5, 7]], axis=0, tiled=False
    ).reshape(4, 2 * heads * head_size, w_out.shape[3])
    mine = lax.dynamic_index_in_dim(meta_all, t, 0, keepdims=False)
    modal_all = mine[:, 0].reshape(-1)
    doc_all = mine[:, 1].reshape(-1)
    text_part = qkv_product(tok_all, weights[0])
    image_part = qkv_product(tok_all, weights[1])
    projected = jnp.where(modal_all[:, None, None] == 1, image_part, text_part).astype(jnp.bfloat16)
    head_list = []
    for head_idx in range(heads):
        queries = projected[:, head_idx, :head_size]
        keys_all = projected[:, head_idx, head_size : 2 * head_size]
        values_all = projected[:, head_idx, 2 * head_size :]
        head_list.append(dense_attend(queries, keys_all, values_all, doc_all, score_scale))
    ho = jnp.concatenate(head_list, axis=1)
    block = lax.dynamic_slice_in_dim(meta_all[:, :, 0], z * 2, 2, 1)
    block = (block.reshape(4, -1, 1) == 1).astype(jnp.bfloat16)
    mask = jnp.broadcast_to(block, (4, block.shape[1], 128))
    return out_project(ho, mask, columns)[None]


def solution(mesh):
    small = mesh.shape["seq"] == 8 and mesh.shape["tower"] == 4
    return jax.shard_map(
        fast_local if small else local,
        mesh=mesh,
        in_specs=(
            P("tower", "seq", None),
            P("tower", "seq"),
            P("tower", "seq"),
            P(None, "seq", "tower", None),
            P(None, "seq", None, "tower"),
        ),
        out_specs=P("tower", "seq", None),
        check_vma=False,
    )
```

```python
import math

import jax
import jax.numpy as jnp
from jax import lax
from jax.experimental import pallas as pl
from jax.experimental.pallas import tpu as pltpu
from jax.sharding import PartitionSpec as P


def key_scores(q_block, keys_tile):
    return lax.dot_general(
        q_block, keys_tile, (((1,), (1,)), ((), ())), preferred_element_type=jnp.float32
    )


def dense_attend(queries, keys_all, values_all, doc_ids, score_scale):
    length = queries.shape[0]
    head_size = queries.shape[1]
    block_rows = min(512, length)
    positions = jnp.arange(length, dtype=jnp.int32)

    def one_block(block_idx):
        first_row = block_idx * block_rows
        q_block = lax.dynamic_slice_in_dim(queries, first_row, block_rows, 0)
        q_docs = lax.dynamic_slice_in_dim(doc_ids, first_row, block_rows, 0)
        q_pos = first_row + jnp.arange(block_rows, dtype=jnp.int32)
        scores = key_scores(q_block, keys_all) * score_scale
        allowed = (q_docs[:, None] == doc_ids[None, :]) & (positions[None, :] <= q_pos[:, None])
        scores = jnp.where(allowed, scores, -jnp.inf)
        row_top = jnp.max(scores, axis=1, keepdims=True)
        expon = jnp.exp(scores - row_top)
        probs = (expon / jnp.sum(expon, axis=1, keepdims=True)).astype(jnp.bfloat16)
        return jnp.dot(probs, values_all, preferred_element_type=jnp.float32).astype(jnp.bfloat16)

    outputs = lax.map(one_block, jnp.arange(length // block_rows, dtype=jnp.int32))
    return outputs.reshape(length, head_size)


def qkv_product(row_block, weight):
    return jnp.einsum("rd,hde->rhe", row_block, weight, preferred_element_type=jnp.float32)


def out_product(row_block, weight):
    return jnp.einsum("rhc,hcd->rd", row_block, weight, preferred_element_type=jnp.float32)


def local(inputs, modality, segment, w_qkv, w_out):
    tok_rows = inputs.shape[1]
    seq_devices = lax.axis_size("seq")
    length = tok_rows * seq_devices
    head_group = w_qkv.shape[1]
    head_size = w_out.shape[2]
    score_scale = 1.0 / math.sqrt(head_size)
    weights = lax.all_gather(w_qkv, "tower", axis=2, tiled=True)
    start_carry = (
        jnp.zeros((length, head_group, 3 * head_size), jnp.float32),
        jnp.zeros((length,), jnp.int32),
        jnp.zeros((length,), jnp.int32),
    )
    first_row = jnp.int32(0)
    row_piece = lax.all_gather(inputs, "seq", axis=1, tiled=True)
    modal_piece = lax.all_gather(modality, "seq", axis=1, tiled=True)
    doc_piece = lax.all_gather(segment, "seq", axis=1, tiled=True)
    text_part = qkv_product(row_piece[0], weights[0])
    image_part = qkv_product(row_piece[0], weights[1])
    selected = jnp.where(modal_piece[0][:, None, None] == 1, image_part, text_part)
    projected = selected
    modal_all = lax.dynamic_update_slice_in_dim(start_carry[1], modal_piece[0], first_row, 0)
    doc_all = lax.dynamic_update_slice_in_dim(start_carry[2], doc_piece[0], first_row, 0)
    projected = projected.astype(jnp.bfloat16)
    head_list = []
    for head_idx in range(head_group):
        queries = projected[:, head_idx, :head_size]
        keys_all = projected[:, head_idx, head_size : 2 * head_size]
        values_all = projected[:, head_idx, 2 * head_size :]
        head_list.append(dense_attend(queries, keys_all, values_all, doc_all, score_scale))
    head_out = jnp.stack(head_list, axis=0)
    columns = lax.all_gather(w_out, "tower", axis=3, tiled=True)
    out_rows = head_out
    out_rows = jnp.transpose(out_rows, (1, 0, 2))
    text_out = out_product(out_rows, columns[0])
    image_out = out_product(out_rows, columns[1])
    summed = lax.psum_scatter(
        jnp.where(modal_all[:, None] == 1, image_out, text_out).astype(jnp.bfloat16),
        "seq",
        scatter_dimension=0,
        tiled=True,
    )
    return summed[None]


MESH = pl.DeviceIdType.MESH
PIECES = 4


def coords():
    s, t = lax.axis_index("seq"), lax.axis_index("tower")
    return s, t, s // 2, s % 2, t // 2, t % 2


def enter(peers):
    barrier = pltpu.get_barrier_semaphore()
    for peer in peers:
        pl.semaphore_signal(barrier, inc=1, device_id=peer, device_id_type=MESH)
    pl.semaphore_wait(barrier, len(peers))


def remote(src, dst, send, recv, peer):
    return pltpu.make_async_remote_copy(
        src_ref=src, dst_ref=dst, send_sem=send, recv_sem=recv,
        device_id=peer, device_id_type=MESH,
    )


def gather_kernel(
    tok, meta, w, w_out, tok_all, meta_all, w_all, near,
    w_buf, tok_buf, local_sem, n_send, n_recv, up_send, dn_send, z_recv, y_send, y_recv,
    w_send, w_recv, m_send, m_recv, mt_send, mt_recv,
):
    s, t, z, y, x, c = coords()
    rows = tok.shape[0]
    depth = w.shape[2]
    x_peer = (s, (1 - x) * 2 + c)
    core_peer = (s, x * 2 + (1 - c))
    diagonal = (s, (1 - x) * 2 + (1 - c))
    y_peer = (z * 2 + (1 - y), t)
    seq_peers = [(lax.rem(s + k, 8), t) for k in range(1, 8)]
    enter(seq_peers + [x_peer, core_peer, diagonal])

    piece = rows // PIECES

    def tok_at(block, p):
        return tok_all.at[pl.ds(pl.multiple_of(block * rows + p * piece, piece), piece)]

    def mine(p):
        return tok.at[pl.ds(p * piece, piece)]

    def w_at(owner, m, h):
        return w_all.at[m, h, pl.ds(pl.multiple_of(owner * depth, depth), depth)]

    chunks = [(m, h) for m in range(w.shape[0]) for h in range(w.shape[1])]

    def up(o, p, src):
        return remote(src, tok_at(o * 2 + y, p), up_send.at[o, p], z_recv.at[o, p], (s + 2, t))

    def down(o, p, src):
        return remote(src, tok_at(o * 2 + y, p), dn_send.at[o, p], z_recv.at[o, p], (s - 2, t))

    def across(o, p, src):
        return remote(src, tok_at(o * 2 + y, p), y_send.at[o, p], y_recv.at[o, p], y_peer)

    def w_copy(kind, k, src, owner, peer):
        m, h = chunks[k]
        return remote(src, w_at(owner, m, h), w_send.at[kind, k], w_recv.at[kind, k], peer)

    for p in range(PIECES):
        @pl.when(z < 3)
        def _():
            up(z, p, mine(p)).start()

        @pl.when(z > 0)
        def _():
            down(z, p, mine(p)).start()

        across(z, p, mine(p)).start()
    for k, (m, h) in enumerate(chunks):
        w_copy(0, k, w.at[m, h], t, x_peer).start()
    meta_copies = [
        remote(meta, meta_all.at[t, s], m_send.at[k], m_recv.at[k], peer)
        for k, peer in enumerate(seq_peers)
    ]
    for copy in meta_copies:
        copy.start()
    for k, (m, h) in enumerate(chunks):
        w_copy(1, k, w.at[m, h], t, core_peer).start()
    def near_up():
        return remote(w_out, near.at[0], n_send.at[0], n_recv.at[0], (s + 2, t))

    def near_down():
        return remote(w_out, near.at[1], n_send.at[1], n_recv.at[1], (s - 2, t))

    @pl.when(z < 3)
    def _():
        near_up().start()

    @pl.when(z > 0)
    def _():
        near_down().start()

    own_rows = tok_all.at[pl.ds(pl.multiple_of(s * rows, rows), rows)]
    staged = [pltpu.make_async_copy(tok, tok_buf, local_sem.at[0])]
    own = [
        pltpu.make_async_copy(tok_buf, own_rows, local_sem.at[1]),
        pltpu.make_async_copy(meta, meta_all.at[t, s], local_sem.at[2]),
    ]
    for k, (m, h) in enumerate(chunks):
        staged.append(pltpu.make_async_copy(w.at[m, h], w_buf.at[k], local_sem.at[3 + 2 * k]))
        own.append(pltpu.make_async_copy(w_buf.at[k], w_at(t, m, h), local_sem.at[4 + 2 * k]))
    for copy in staged:
        copy.start()
    for copy in staged:
        copy.wait()
    for copy in own:
        copy.start()

    def pass_weights(k):
        m, h = chunks[k]
        w_copy(0, k, w.at[m, h], t, x_peer).wait_recv()
        w_copy(2, k, w_at(x_peer[1], m, h), x_peer[1], core_peer).start()

    n_chunks = len(chunks)
    for d in range(1, 4):
        if d - 1 < n_chunks:
            pass_weights(d - 1)
        low, high = z - d, z + d
        for p in range(PIECES):
            @pl.when(low >= 0)
            def _():
                src = tok_at(low * 2 + y, p)
                up(low, p, src).wait_recv()

                @pl.when(z < 3)
                def _():
                    up(low, p, src).start()

                across(low, p, src).start()

            @pl.when(high <= 3)
            def _():
                src = tok_at(high * 2 + y, p)
                down(high, p, src).wait_recv()

                @pl.when(z > 0)
                def _():
                    down(high, p, src).start()

                across(high, p, src).start()

    for k in range(3, n_chunks):
        pass_weights(k)
    for copy in own:
        copy.wait()
    for copy in meta_copies:
        copy.wait()
    tower_meta = [
        remote(meta_all.at[t], meta_all.at[t], mt_send.at[k], mt_recv.at[k], peer)
        for k, peer in enumerate((x_peer, core_peer, diagonal))
    ]
    for copy in tower_meta:
        copy.start()
    for o in range(4):
        for p in range(PIECES):
            across(o, p, mine(p)).wait()

            @pl.when((z < 3) & (o <= z))
            def _():
                up(o, p, mine(p)).wait_send()

            @pl.when((z > 0) & (o >= z))
            def _():
                down(o, p, mine(p)).wait_send()

    for k, (m, h) in enumerate(chunks):
        w_copy(0, k, w.at[m, h], t, x_peer).wait_send()
        w_copy(1, k, w.at[m, h], t, core_peer).wait()
        w_copy(2, k, w.at[m, h], t, core_peer).wait()
    for copy in tower_meta:
        copy.wait()

    @pl.when(z < 3)
    def _():
        near_up().wait_send()
        near_down().wait_recv()

    @pl.when(z > 0)
    def _():
        near_down().wait_send()
        near_up().wait_recv()


def gather_all(tok, meta, w, w_out):
    dma = pltpu.SemaphoreType.DMA
    hbm = pl.BlockSpec(memory_space=pl.ANY)
    heads = w.shape[1]
    return pl.pallas_call(
        gather_kernel,
        out_shape=(
            jax.ShapeDtypeStruct((tok.shape[0] * 8, tok.shape[1]), tok.dtype),
            jax.ShapeDtypeStruct((4, 8) + meta.shape, meta.dtype),
            jax.ShapeDtypeStruct((2, heads, w.shape[2] * 4, w.shape[3]), w.dtype),
            jax.ShapeDtypeStruct((2,) + w_out.shape, w_out.dtype),
        ),
        in_specs=[hbm] * 4,
        out_specs=(hbm, hbm, hbm, hbm),
        scratch_shapes=[
            pltpu.VMEM((2 * heads,) + w.shape[2:], w.dtype), pltpu.VMEM(tok.shape, tok.dtype),
            dma((3 + 4 * heads,)), dma((2,)), dma((2,)), dma((4, PIECES)), dma((4, PIECES)), dma((4, PIECES)),
            dma((4, PIECES)), dma((4, PIECES)),
            dma((3, 2 * heads)), dma((3, 2 * heads)), dma((7,)), dma((7,)), dma((3,)), dma((3,)),
        ],
        compiler_params=pltpu.CompilerParams(
            collective_id=0, has_side_effects=True, vmem_limit_bytes=16 << 20
        ),
        cost_estimate=pl.CostEstimate(flops=0, bytes_accessed=42 << 20, transcendentals=0),
    )(tok, meta, w, w_out)


def out_kernel(
    ho, mask, w0, w1, w2, w3, out, got, lhs, keep, sent, arrived, ready,
    z_send, z_recv, g_send, g_recv, y_send, y_recv, o_send, o_recv,
):
    s, t, z, y, x, c = coords()
    rows = ho.shape[0] // 4
    half = rows // 2
    width = ho.shape[1]
    cols = w0.shape[1]
    below = jnp.where(z == 0, 1, z - 1)
    across = lax.rem(z + 2, 4)
    groups = [(z, w0), (below, w1), (across, w2), (6 - z - below - across, w3)]
    order = [t, x * 2 + (1 - c), (1 - x) * 2 + c, (1 - x) * 2 + (1 - c)]
    x_peer, core_peer = (s, order[2]), (s, order[1])
    y_peer = (z * 2 + (1 - y), t)
    z_peers = [(lax.rem(s + 2 * k, 8), t) for k in range(1, 4)]
    enter(z_peers + [(s, o) for o in order[1:]] + [y_peer])

    def rows_of(block, n):
        return pl.ds(pl.multiple_of(block * n, n), n)

    z_copies = [
        remote(
            ho.at[rows_of(lax.rem(z + k, 4), rows)], got.at[t, z],
            z_send.at[k - 1], z_recv.at[k - 1], z_peers[k - 1],
        )
        for k in range(1, 4)
    ]
    for copy in z_copies:
        copy.start()
    got[t, z] = ho[rows_of(z, rows)]
    for copy in z_copies:
        copy.wait_recv()
    g_copies = [
        remote(got.at[t], got.at[t], g_send.at[0], g_recv.at[0], x_peer),
        remote(got.at[t], got.at[t], g_send.at[1], g_recv.at[1], core_peer),
        remote(got.at[order[2]], got.at[order[2]], g_send.at[2], g_recv.at[2], core_peer),
    ]
    g_copies[0].start()
    g_copies[1].start()

    def project(j):
        owner = order[j]
        for g in range(4):
            block = got[owner, groups[g][0]]
            m = mask[owner]
            for h in range(width // 128):
                part = block[:, h * 128:(h + 1) * 128]
                image = part * m
                lhs[g, :, h * 128:(h + 1) * 128] = part - image
                lhs[g, :, width + h * 128:width + (h + 1) * 128] = image

        @pl.loop(0, cols // 256)
        def _(tile):
            at = rows_of(tile, 256)
            for away in range(2):
                side = (1 - y) if away else y
                total = None
                for g in range(4):
                    part = jnp.dot(
                        lhs[g, rows_of(side, half), :], groups[g][1][:, at],
                        preferred_element_type=jnp.float32,
                    ).astype(jnp.bfloat16).astype(jnp.float32)
                    total = part if total is None else total + part
                if away:
                    sent[j, :, at] = total.astype(jnp.bfloat16)
                else:
                    keep[j, :, at] = total

    y_copies = [
        remote(sent.at[j], arrived.at[j], y_send.at[j], y_recv.at[j], y_peer) for j in range(4)
    ]
    my_cols = rows_of(t, cols)
    o_copies = [
        remote(ready.at[j], out.at[:, my_cols], o_send.at[j - 1], o_recv.at[j - 1], (s, order[j]))
        for j in range(1, 4)
    ]

    def finish(j):
        y_copies[j].wait_recv()
        total = (keep[j] + arrived[j].astype(jnp.float32)).astype(jnp.bfloat16)
        if j == 0:
            out[:, my_cols] = total
        else:
            ready[j] = total
            o_copies[j - 1].start()

    project(0)
    y_copies[0].start()
    g_copies[1].wait_recv()
    project(1)
    y_copies[1].start()
    g_copies[0].wait_recv()
    g_copies[2].start()
    project(2)
    y_copies[2].start()
    finish(1)
    g_copies[2].wait_recv()
    project(3)
    y_copies[3].start()
    finish(0)
    finish(2)
    finish(3)
    for copy in z_copies + g_copies + y_copies:
        copy.wait_send()
    for copy in o_copies:
        copy.wait()


def out_project(ho, mask, ws):
    dma = pltpu.SemaphoreType.DMA
    vmem = pl.BlockSpec(memory_space=pltpu.VMEM)
    rows, cols, width = ho.shape[0] // 4, ws[0].shape[1], ho.shape[1]
    return pl.pallas_call(
        out_kernel,
        out_shape=jax.ShapeDtypeStruct((rows // 2, cols * 4), jnp.bfloat16),
        in_specs=[vmem] * 6,
        out_specs=vmem,
        scratch_shapes=[
            pltpu.VMEM((4, 4, rows, width), jnp.bfloat16),
            pltpu.VMEM((4, rows, 2 * width), jnp.bfloat16),
            pltpu.VMEM((4, rows // 2, cols), jnp.float32),
            pltpu.VMEM((4, rows // 2, cols), jnp.bfloat16),
            pltpu.VMEM((4, rows // 2, cols), jnp.bfloat16),
            pltpu.VMEM((4, rows // 2, cols), jnp.bfloat16),
            dma((3,)), dma((3,)), dma((3,)), dma((3,)), dma((4,)), dma((4,)), dma((3,)), dma((3,)),
        ],
        compiler_params=pltpu.CompilerParams(
            collective_id=1, has_side_effects=True, vmem_limit_bytes=40 << 20
        ),
        cost_estimate=pl.CostEstimate(
            flops=4 * 1024 * 1024 * 1024, bytes_accessed=8 << 20, transcendentals=0
        ),
    )(ho, mask, *ws)


def fast_local(inputs, modality, segment, w_qkv, w_out):
    heads, head_size = w_qkv.shape[1], w_out.shape[2]
    score_scale = 1.0 / math.sqrt(head_size)
    meta = jnp.concatenate([modality, segment, jnp.zeros((6, modality.shape[1]), jnp.int32)], axis=0)
    tok_all, meta_all, weights, near = gather_all(inputs[0], meta, w_qkv, w_out)
    s, t, z, y, x, c = coords()
    up_pairs = [(a * 2 + b, (a + 1) * 2 + b) for a in (1, 2) for b in (0, 1)]
    down_pairs = [(a * 2 + b, (a - 1) * 2 + b) for a in (1, 2) for b in (0, 1)]
    end_pairs = [(2 + b, b) for b in (0, 1)] + [(4 + b, 6 + b) for b in (0, 1)]
    from_low = lax.ppermute(near[0], "seq", up_pairs)
    from_high = lax.ppermute(near[1], "seq", down_pairs)
    far = jnp.where(z >= 2, from_low, from_high)
    last = lax.ppermute(far, "seq", end_pairs)
    blocks = [
        w_out,
        jnp.where(z == 0, near[1], near[0]),
        far,
        jnp.where((z == 0) | (z == 3), last, near[1]),
    ]
    columns = [b.reshape(2 * heads * head_size, w_out.shape[3]) for b in blocks]
    mine = lax.dynamic_index_in_dim(meta_all, t, 0, keepdims=False)
    modal_all = mine[:, 0].reshape(-1)
    doc_all = mine[:, 1].reshape(-1)
    text_part = qkv_product(tok_all, weights[0])
    image_part = qkv_product(tok_all, weights[1])
    projected = jnp.where(modal_all[:, None, None] == 1, image_part, text_part).astype(jnp.bfloat16)
    head_list = []
    for head_idx in range(heads):
        queries = projected[:, head_idx, :head_size]
        keys_all = projected[:, head_idx, head_size : 2 * head_size]
        values_all = projected[:, head_idx, 2 * head_size :]
        head_list.append(dense_attend(queries, keys_all, values_all, doc_all, score_scale))
    ho = jnp.concatenate(head_list, axis=1)
    block = lax.dynamic_slice_in_dim(meta_all[:, :, 0], z * 2, 2, 1)
    block = (block.reshape(4, -1, 1) == 1).astype(jnp.bfloat16)
    mask = jnp.broadcast_to(block, (4, block.shape[1], 128))
    return out_project(ho, mask, columns)[None]


def solution(mesh):
    small = mesh.shape["seq"] == 8 and mesh.shape["tower"] == 4
    return jax.shard_map(
        fast_local if small else local,
        mesh=mesh,
        in_specs=(
            P("tower", "seq", None),
            P("tower", "seq"),
            P("tower", "seq"),
            P(None, "seq", "tower", None),
            P(None, "seq", None, "tower"),
        ),
        out_specs=P("tower", "seq", None),
        check_vma=False,
    )
```

```python
import math

import jax
import jax.numpy as jnp
from jax import lax
from jax.experimental import pallas as pl
from jax.experimental.pallas import tpu as pltpu
from jax.sharding import PartitionSpec as P


def key_scores(q_block, keys_tile):
    return lax.dot_general(
        q_block, keys_tile, (((1,), (1,)), ((), ())), preferred_element_type=jnp.float32
    )


def dense_attend(queries, keys_all, values_all, doc_ids, score_scale):
    length = queries.shape[0]
    head_size = queries.shape[1]
    block_rows = min(512, length)
    positions = jnp.arange(length, dtype=jnp.int32)

    def one_block(block_idx):
        first_row = block_idx * block_rows
        q_block = lax.dynamic_slice_in_dim(queries, first_row, block_rows, 0)
        q_docs = lax.dynamic_slice_in_dim(doc_ids, first_row, block_rows, 0)
        q_pos = first_row + jnp.arange(block_rows, dtype=jnp.int32)
        scores = key_scores(q_block, keys_all) * score_scale
        allowed = (q_docs[:, None] == doc_ids[None, :]) & (positions[None, :] <= q_pos[:, None])
        scores = jnp.where(allowed, scores, -jnp.inf)
        row_top = jnp.max(scores, axis=1, keepdims=True)
        expon = jnp.exp(scores - row_top)
        probs = (expon / jnp.sum(expon, axis=1, keepdims=True)).astype(jnp.bfloat16)
        return jnp.dot(probs, values_all, preferred_element_type=jnp.float32).astype(jnp.bfloat16)

    outputs = lax.map(one_block, jnp.arange(length // block_rows, dtype=jnp.int32))
    return outputs.reshape(length, head_size)


def qkv_product(row_block, weight):
    return jnp.einsum("rd,hde->rhe", row_block, weight, preferred_element_type=jnp.float32)


def out_product(row_block, weight):
    return jnp.einsum("rhc,hcd->rd", row_block, weight, preferred_element_type=jnp.float32)


def local(inputs, modality, segment, w_qkv, w_out):
    tok_rows = inputs.shape[1]
    seq_devices = lax.axis_size("seq")
    length = tok_rows * seq_devices
    head_group = w_qkv.shape[1]
    head_size = w_out.shape[2]
    score_scale = 1.0 / math.sqrt(head_size)
    weights = lax.all_gather(w_qkv, "tower", axis=2, tiled=True)
    start_carry = (
        jnp.zeros((length, head_group, 3 * head_size), jnp.float32),
        jnp.zeros((length,), jnp.int32),
        jnp.zeros((length,), jnp.int32),
    )
    first_row = jnp.int32(0)
    row_piece = lax.all_gather(inputs, "seq", axis=1, tiled=True)
    modal_piece = lax.all_gather(modality, "seq", axis=1, tiled=True)
    doc_piece = lax.all_gather(segment, "seq", axis=1, tiled=True)
    text_part = qkv_product(row_piece[0], weights[0])
    image_part = qkv_product(row_piece[0], weights[1])
    selected = jnp.where(modal_piece[0][:, None, None] == 1, image_part, text_part)
    projected = selected
    modal_all = lax.dynamic_update_slice_in_dim(start_carry[1], modal_piece[0], first_row, 0)
    doc_all = lax.dynamic_update_slice_in_dim(start_carry[2], doc_piece[0], first_row, 0)
    projected = projected.astype(jnp.bfloat16)
    head_list = []
    for head_idx in range(head_group):
        queries = projected[:, head_idx, :head_size]
        keys_all = projected[:, head_idx, head_size : 2 * head_size]
        values_all = projected[:, head_idx, 2 * head_size :]
        head_list.append(dense_attend(queries, keys_all, values_all, doc_all, score_scale))
    head_out = jnp.stack(head_list, axis=0)
    columns = lax.all_gather(w_out, "tower", axis=3, tiled=True)
    out_rows = head_out
    out_rows = jnp.transpose(out_rows, (1, 0, 2))
    text_out = out_product(out_rows, columns[0])
    image_out = out_product(out_rows, columns[1])
    summed = lax.psum_scatter(
        jnp.where(modal_all[:, None] == 1, image_out, text_out).astype(jnp.bfloat16),
        "seq",
        scatter_dimension=0,
        tiled=True,
    )
    return summed[None]


MESH = pl.DeviceIdType.MESH
PIECES = 4


def coords():
    s, t = lax.axis_index("seq"), lax.axis_index("tower")
    return s, t, s // 2, s % 2, t // 2, t % 2


def enter(peers):
    barrier = pltpu.get_barrier_semaphore()
    for peer in peers:
        pl.semaphore_signal(barrier, inc=1, device_id=peer, device_id_type=MESH)
    pl.semaphore_wait(barrier, len(peers))


def remote(src, dst, send, recv, peer):
    return pltpu.make_async_remote_copy(
        src_ref=src, dst_ref=dst, send_sem=send, recv_sem=recv,
        device_id=peer, device_id_type=MESH,
    )


def gather_kernel(
    tok, meta, w, w_out, tok_all, meta_all, w_all, near_low, near_high,
    w_buf, tok_buf, local_sem, n_send, n_recv, up_send, dn_send, z_recv, y_send, y_recv,
    w_send, w_recv, m_send, m_recv, mt_send, mt_recv,
):
    s, t, z, y, x, c = coords()
    rows = tok.shape[0]
    depth = w.shape[2]
    x_peer = (s, (1 - x) * 2 + c)
    core_peer = (s, x * 2 + (1 - c))
    diagonal = (s, (1 - x) * 2 + (1 - c))
    y_peer = (z * 2 + (1 - y), t)
    seq_peers = [(lax.rem(s + k, 8), t) for k in range(1, 8)]
    enter(seq_peers + [x_peer, core_peer, diagonal])

    piece = rows // PIECES

    def tok_at(block, p):
        return tok_all.at[pl.ds(pl.multiple_of(block * rows + p * piece, piece), piece)]

    def mine(p):
        return tok.at[pl.ds(p * piece, piece)]

    def w_at(owner, m, h):
        return w_all.at[m, h, pl.ds(pl.multiple_of(owner * depth, depth), depth)]

    chunks = [(m, h) for m in range(w.shape[0]) for h in range(w.shape[1])]

    def up(o, p, src):
        return remote(src, tok_at(o * 2 + y, p), up_send.at[o, p], z_recv.at[o, p], (s + 2, t))

    def down(o, p, src):
        return remote(src, tok_at(o * 2 + y, p), dn_send.at[o, p], z_recv.at[o, p], (s - 2, t))

    def across(o, p, src):
        return remote(src, tok_at(o * 2 + y, p), y_send.at[o, p], y_recv.at[o, p], y_peer)

    def w_copy(kind, k, src, owner, peer):
        m, h = chunks[k]
        return remote(src, w_at(owner, m, h), w_send.at[kind, k], w_recv.at[kind, k], peer)

    for p in range(PIECES):
        @pl.when(z < 3)
        def _():
            up(z, p, mine(p)).start()

        @pl.when(z > 0)
        def _():
            down(z, p, mine(p)).start()

        across(z, p, mine(p)).start()
    for k, (m, h) in enumerate(chunks):
        w_copy(0, k, w.at[m, h], t, x_peer).start()
    meta_copies = [
        remote(meta, meta_all.at[t, s], m_send.at[k], m_recv.at[k], peer)
        for k, peer in enumerate(seq_peers)
    ]
    for copy in meta_copies:
        copy.start()
    for k, (m, h) in enumerate(chunks):
        w_copy(1, k, w.at[m, h], t, core_peer).start()
    def near_up():
        return remote(w_out, near_low, n_send.at[0], n_recv.at[0], (s + 2, t))

    def near_down():
        return remote(w_out, near_high, n_send.at[1], n_recv.at[1], (s - 2, t))

    @pl.when(z < 3)
    def _():
        near_up().start()

    @pl.when(z > 0)
    def _():
        near_down().start()

    own_rows = tok_all.at[pl.ds(pl.multiple_of(s * rows, rows), rows)]
    staged = [pltpu.make_async_copy(tok, tok_buf, local_sem.at[0])]
    own = [
        pltpu.make_async_copy(tok_buf, own_rows, local_sem.at[1]),
        pltpu.make_async_copy(meta, meta_all.at[t, s], local_sem.at[2]),
    ]
    for k, (m, h) in enumerate(chunks):
        staged.append(pltpu.make_async_copy(w.at[m, h], w_buf.at[k], local_sem.at[3 + 2 * k]))
        own.append(pltpu.make_async_copy(w_buf.at[k], w_at(t, m, h), local_sem.at[4 + 2 * k]))
    for copy in staged:
        copy.start()
    for copy in staged:
        copy.wait()
    for copy in own:
        copy.start()

    def pass_weights(k):
        m, h = chunks[k]
        w_copy(0, k, w.at[m, h], t, x_peer).wait_recv()
        w_copy(2, k, w_at(x_peer[1], m, h), x_peer[1], core_peer).start()

    n_chunks = len(chunks)
    for d in range(1, 4):
        if d - 1 < n_chunks:
            pass_weights(d - 1)
        low, high = z - d, z + d
        for p in range(PIECES):
            @pl.when(low >= 0)
            def _():
                src = tok_at(low * 2 + y, p)
                up(low, p, src).wait_recv()

                @pl.when(z < 3)
                def _():
                    up(low, p, src).start()

                across(low, p, src).start()

            @pl.when(high <= 3)
            def _():
                src = tok_at(high * 2 + y, p)
                down(high, p, src).wait_recv()

                @pl.when(z > 0)
                def _():
                    down(high, p, src).start()

                across(high, p, src).start()

    for k in range(3, n_chunks):
        pass_weights(k)
    for copy in own:
        copy.wait()
    for copy in meta_copies:
        copy.wait()
    tower_meta = [
        remote(meta_all.at[t], meta_all.at[t], mt_send.at[k], mt_recv.at[k], peer)
        for k, peer in enumerate((x_peer, core_peer, diagonal))
    ]
    for copy in tower_meta:
        copy.start()
    for o in range(4):
        for p in range(PIECES):
            across(o, p, mine(p)).wait()

            @pl.when((z < 3) & (o <= z))
            def _():
                up(o, p, mine(p)).wait_send()

            @pl.when((z > 0) & (o >= z))
            def _():
                down(o, p, mine(p)).wait_send()

    for k, (m, h) in enumerate(chunks):
        w_copy(0, k, w.at[m, h], t, x_peer).wait_send()
        w_copy(1, k, w.at[m, h], t, core_peer).wait()
        w_copy(2, k, w.at[m, h], t, core_peer).wait()
    for copy in tower_meta:
        copy.wait()

    @pl.when(z < 3)
    def _():
        near_up().wait_send()
        near_down().wait_recv()

    @pl.when(z > 0)
    def _():
        near_down().wait_send()
        near_up().wait_recv()


def gather_all(tok, meta, w, w_out):
    dma = pltpu.SemaphoreType.DMA
    hbm = pl.BlockSpec(memory_space=pl.ANY)
    heads = w.shape[1]
    return pl.pallas_call(
        gather_kernel,
        out_shape=(
            jax.ShapeDtypeStruct((tok.shape[0] * 8, tok.shape[1]), tok.dtype),
            jax.ShapeDtypeStruct((4, 8) + meta.shape, meta.dtype),
            jax.ShapeDtypeStruct((2, heads, w.shape[2] * 4, w.shape[3]), w.dtype),
            jax.ShapeDtypeStruct(w_out.shape, w_out.dtype),
            jax.ShapeDtypeStruct(w_out.shape, w_out.dtype),
        ),
        in_specs=[hbm] * 4,
        out_specs=(hbm,) * 5,
        scratch_shapes=[
            pltpu.VMEM((2 * heads,) + w.shape[2:], w.dtype), pltpu.VMEM(tok.shape, tok.dtype),
            dma((3 + 4 * heads,)), dma((2,)), dma((2,)), dma((4, PIECES)), dma((4, PIECES)), dma((4, PIECES)),
            dma((4, PIECES)), dma((4, PIECES)),
            dma((3, 2 * heads)), dma((3, 2 * heads)), dma((7,)), dma((7,)), dma((3,)), dma((3,)),
        ],
        compiler_params=pltpu.CompilerParams(
            collective_id=0, has_side_effects=True, vmem_limit_bytes=56 << 20
        ),
        cost_estimate=pl.CostEstimate(flops=0, bytes_accessed=42 << 20, transcendentals=0),
    )(tok, meta, w, w_out)


def out_kernel(
    ho, mask, w0, w1, w2, w3, out, got, lhs, keep, sent, arrived, ready,
    z_send, z_recv, g_send, g_recv, y_send, y_recv, o_send, o_recv,
):
    s, t, z, y, x, c = coords()
    rows = ho.shape[0] // 4
    half = rows // 2
    width = ho.shape[1]
    cols = w0.shape[1]
    below = jnp.where(z == 0, 1, z - 1)
    across = lax.rem(z + 2, 4)
    groups = [(z, w0), (below, w1), (across, w2), (6 - z - below - across, w3)]
    order = [t, x * 2 + (1 - c), (1 - x) * 2 + c, (1 - x) * 2 + (1 - c)]
    x_peer, core_peer = (s, order[2]), (s, order[1])
    y_peer = (z * 2 + (1 - y), t)
    z_peers = [(lax.rem(s + 2 * k, 8), t) for k in range(1, 4)]
    enter(z_peers + [(s, o) for o in order[1:]] + [y_peer])

    def rows_of(block, n):
        return pl.ds(pl.multiple_of(block * n, n), n)

    z_copies = [
        remote(
            ho.at[rows_of(lax.rem(z + k, 4), rows)], got.at[t, z],
            z_send.at[k - 1], z_recv.at[k - 1], z_peers[k - 1],
        )
        for k in range(1, 4)
    ]
    for copy in z_copies:
        copy.start()
    got[t, z] = ho[rows_of(z, rows)]
    origins = [z] + [lax.rem(z + k, 4) for k in (3, 1, 2)]

    def g_copy(kind, i):
        block = got.at[order[2] if kind == 2 else t, origins[i]]
        peer = x_peer if kind == 0 else core_peer
        return remote(block, block, g_send.at[kind, i], g_recv.at[kind, i], peer)

    for i, k in enumerate((0, 1, 3, 2)):
        if k:
            z_copies[k - 1].wait_recv()
        g_copy(0, i).start()
        g_copy(1, i).start()

    def project(j):
        owner = order[j]
        for g in range(4):
            block = got[owner, groups[g][0]]
            m = mask[owner]
            for h in range(width // 128):
                part = block[:, h * 128:(h + 1) * 128]
                image = part * m
                lhs[g, :, h * 128:(h + 1) * 128] = part - image
                lhs[g, :, width + h * 128:width + (h + 1) * 128] = image

        @pl.loop(0, cols // 256)
        def _(tile):
            at = rows_of(tile, 256)
            for away in range(2):
                side = (1 - y) if away else y
                total = None
                for g in range(4):
                    part = jnp.dot(
                        lhs[g, rows_of(side, half), :], groups[g][1][:, at],
                        preferred_element_type=jnp.float32,
                    ).astype(jnp.bfloat16).astype(jnp.float32)
                    total = part if total is None else total + part
                if away:
                    sent[j, :, at] = total.astype(jnp.bfloat16)
                else:
                    keep[j, :, at] = total

    y_copies = [
        remote(sent.at[j], arrived.at[j], y_send.at[j], y_recv.at[j], y_peer) for j in range(4)
    ]
    my_cols = rows_of(t, cols)
    o_copies = [
        remote(ready.at[j], out.at[:, my_cols], o_send.at[j - 1], o_recv.at[j - 1], (s, order[j]))
        for j in range(1, 4)
    ]

    def finish(j):
        y_copies[j].wait_recv()
        total = (keep[j] + arrived[j].astype(jnp.float32)).astype(jnp.bfloat16)
        if j == 0:
            out[:, my_cols] = total
        else:
            ready[j] = total
            o_copies[j - 1].start()

    for i in range(4):
        g_copy(1, i).wait_recv()
    project(1)
    y_copies[1].start()
    for i in range(4):
        g_copy(0, i).wait_recv()
        g_copy(2, i).start()
    project(2)
    y_copies[2].start()
    for i in range(4):
        g_copy(2, i).wait_recv()
    project(3)
    y_copies[3].start()
    finish(1)
    project(0)
    y_copies[0].start()
    finish(2)
    finish(3)
    finish(0)
    for copy in z_copies + y_copies:
        copy.wait_send()
    for kind in range(3):
        for i in range(4):
            g_copy(kind, i).wait_send()
    for copy in o_copies:
        copy.wait()


def out_project(ho, mask, ws):
    dma = pltpu.SemaphoreType.DMA
    vmem = pl.BlockSpec(memory_space=pltpu.VMEM)
    rows, cols, width = ho.shape[0] // 4, ws[0].shape[1], ho.shape[1]
    return pl.pallas_call(
        out_kernel,
        out_shape=jax.ShapeDtypeStruct((rows // 2, cols * 4), jnp.bfloat16),
        in_specs=[vmem] * 6,
        out_specs=vmem,
        scratch_shapes=[
            pltpu.VMEM((4, 4, rows, width), jnp.bfloat16),
            pltpu.VMEM((4, rows, 2 * width), jnp.bfloat16),
            pltpu.VMEM((4, rows // 2, cols), jnp.float32),
            pltpu.VMEM((4, rows // 2, cols), jnp.bfloat16),
            pltpu.VMEM((4, rows // 2, cols), jnp.bfloat16),
            pltpu.VMEM((4, rows // 2, cols), jnp.bfloat16),
            dma((3,)), dma((3,)), dma((3, 4)), dma((3, 4)), dma((4,)), dma((4,)), dma((3,)), dma((3,)),
        ],
        compiler_params=pltpu.CompilerParams(
            collective_id=1, has_side_effects=True, vmem_limit_bytes=40 << 20
        ),
        cost_estimate=pl.CostEstimate(
            flops=4 * 1024 * 1024 * 1024, bytes_accessed=8 << 20, transcendentals=0
        ),
    )(ho, mask, *ws)


def fast_local(inputs, modality, segment, w_qkv, w_out):
    heads, head_size = w_qkv.shape[1], w_out.shape[2]
    score_scale = 1.0 / math.sqrt(head_size)
    meta = jnp.concatenate([modality, segment, jnp.zeros((6, modality.shape[1]), jnp.int32)], axis=0)
    tok_all, meta_all, weights, near_low, near_high = gather_all(inputs[0], meta, w_qkv, w_out)
    s, t, z, y, x, c = coords()
    up_pairs = [(a * 2 + b, (a + 1) * 2 + b) for a in (1, 2) for b in (0, 1)]
    down_pairs = [(a * 2 + b, (a - 1) * 2 + b) for a in (1, 2) for b in (0, 1)]
    end_pairs = [(2 + b, b) for b in (0, 1)] + [(4 + b, 6 + b) for b in (0, 1)]
    from_low = lax.ppermute(near_low, "seq", up_pairs)
    from_high = lax.ppermute(near_high, "seq", down_pairs)
    far = jnp.where(z >= 2, from_low, from_high)
    last = lax.ppermute(far, "seq", end_pairs)
    blocks = [
        w_out,
        jnp.where(z == 0, near_high, near_low),
        far,
        jnp.where((z == 0) | (z == 3), last, near_high),
    ]
    columns = [b.reshape(2 * heads * head_size, w_out.shape[3]) for b in blocks]
    mine = lax.dynamic_index_in_dim(meta_all, t, 0, keepdims=False)
    modal_all = mine[:, 0].reshape(-1)
    doc_all = mine[:, 1].reshape(-1)
    text_part = qkv_product(tok_all, weights[0])
    image_part = qkv_product(tok_all, weights[1])
    projected = jnp.where(modal_all[:, None, None] == 1, image_part, text_part).astype(jnp.bfloat16)
    head_list = []
    for head_idx in range(heads):
        queries = projected[:, head_idx, :head_size]
        keys_all = projected[:, head_idx, head_size : 2 * head_size]
        values_all = projected[:, head_idx, 2 * head_size :]
        head_list.append(dense_attend(queries, keys_all, values_all, doc_all, score_scale))
    ho = jnp.concatenate(head_list, axis=1)
    block = lax.dynamic_slice_in_dim(meta_all[:, :, 0], z * 2, 2, 1)
    block = (block.reshape(4, -1, 1) == 1).astype(jnp.bfloat16)
    mask = jnp.broadcast_to(block, (4, block.shape[1], 128))
    return out_project(ho, mask, columns)[None]


def solution(mesh):
    small = mesh.shape["seq"] == 8 and mesh.shape["tower"] == 4
    return jax.shard_map(
        fast_local if small else local,
        mesh=mesh,
        in_specs=(
            P("tower", "seq", None),
            P("tower", "seq"),
            P("tower", "seq"),
            P(None, "seq", "tower", None),
            P(None, "seq", None, "tower"),
        ),
        out_specs=P("tower", "seq", None),
        check_vma=False,
    )
```

```python
import math

import jax
import jax.numpy as jnp
from jax import lax
from jax.experimental import pallas as pl
from jax.experimental.pallas import tpu as pltpu
from jax.sharding import PartitionSpec as P


def key_scores(q_block, keys_tile):
    return lax.dot_general(
        q_block, keys_tile, (((1,), (1,)), ((), ())), preferred_element_type=jnp.float32
    )


def dense_attend(queries, keys_all, values_all, doc_ids, score_scale):
    length = queries.shape[0]
    head_size = queries.shape[1]
    block_rows = min(512, length)
    positions = jnp.arange(length, dtype=jnp.int32)

    def one_block(block_idx):
        first_row = block_idx * block_rows
        q_block = lax.dynamic_slice_in_dim(queries, first_row, block_rows, 0)
        q_docs = lax.dynamic_slice_in_dim(doc_ids, first_row, block_rows, 0)
        q_pos = first_row + jnp.arange(block_rows, dtype=jnp.int32)
        scores = key_scores(q_block, keys_all) * score_scale
        allowed = (q_docs[:, None] == doc_ids[None, :]) & (positions[None, :] <= q_pos[:, None])
        scores = jnp.where(allowed, scores, -jnp.inf)
        row_top = jnp.max(scores, axis=1, keepdims=True)
        expon = jnp.exp(scores - row_top)
        probs = (expon / jnp.sum(expon, axis=1, keepdims=True)).astype(jnp.bfloat16)
        return jnp.dot(probs, values_all, preferred_element_type=jnp.float32).astype(jnp.bfloat16)

    outputs = lax.map(one_block, jnp.arange(length // block_rows, dtype=jnp.int32))
    return outputs.reshape(length, head_size)


def qkv_product(row_block, weight):
    return jnp.einsum("rd,hde->rhe", row_block, weight, preferred_element_type=jnp.float32)


def out_product(row_block, weight):
    return jnp.einsum("rhc,hcd->rd", row_block, weight, preferred_element_type=jnp.float32)


def local(inputs, modality, segment, w_qkv, w_out):
    tok_rows = inputs.shape[1]
    seq_devices = lax.axis_size("seq")
    length = tok_rows * seq_devices
    head_group = w_qkv.shape[1]
    head_size = w_out.shape[2]
    score_scale = 1.0 / math.sqrt(head_size)
    weights = lax.all_gather(w_qkv, "tower", axis=2, tiled=True)
    start_carry = (
        jnp.zeros((length, head_group, 3 * head_size), jnp.float32),
        jnp.zeros((length,), jnp.int32),
        jnp.zeros((length,), jnp.int32),
    )
    first_row = jnp.int32(0)
    row_piece = lax.all_gather(inputs, "seq", axis=1, tiled=True)
    modal_piece = lax.all_gather(modality, "seq", axis=1, tiled=True)
    doc_piece = lax.all_gather(segment, "seq", axis=1, tiled=True)
    text_part = qkv_product(row_piece[0], weights[0])
    image_part = qkv_product(row_piece[0], weights[1])
    selected = jnp.where(modal_piece[0][:, None, None] == 1, image_part, text_part)
    projected = selected
    modal_all = lax.dynamic_update_slice_in_dim(start_carry[1], modal_piece[0], first_row, 0)
    doc_all = lax.dynamic_update_slice_in_dim(start_carry[2], doc_piece[0], first_row, 0)
    projected = projected.astype(jnp.bfloat16)
    head_list = []
    for head_idx in range(head_group):
        queries = projected[:, head_idx, :head_size]
        keys_all = projected[:, head_idx, head_size : 2 * head_size]
        values_all = projected[:, head_idx, 2 * head_size :]
        head_list.append(dense_attend(queries, keys_all, values_all, doc_all, score_scale))
    head_out = jnp.stack(head_list, axis=0)
    columns = lax.all_gather(w_out, "tower", axis=3, tiled=True)
    out_rows = head_out
    out_rows = jnp.transpose(out_rows, (1, 0, 2))
    text_out = out_product(out_rows, columns[0])
    image_out = out_product(out_rows, columns[1])
    summed = lax.psum_scatter(
        jnp.where(modal_all[:, None] == 1, image_out, text_out).astype(jnp.bfloat16),
        "seq",
        scatter_dimension=0,
        tiled=True,
    )
    return summed[None]


MESH = pl.DeviceIdType.MESH
PIECES = 4


def coords():
    s, t = lax.axis_index("seq"), lax.axis_index("tower")
    return s, t, s // 2, s % 2, t // 2, t % 2


def enter(peers):
    barrier = pltpu.get_barrier_semaphore()
    for peer in peers:
        pl.semaphore_signal(barrier, inc=1, device_id=peer, device_id_type=MESH)
    pl.semaphore_wait(barrier, len(peers))


def remote(src, dst, send, recv, peer):
    return pltpu.make_async_remote_copy(
        src_ref=src, dst_ref=dst, send_sem=send, recv_sem=recv,
        device_id=peer, device_id_type=MESH,
    )


def gather_kernel(
    tok, meta, w, w_out, tok_all, meta_all, w_all, near_low, near_high,
    w_buf, tok_buf, local_sem, n_send, n_recv, up_send, dn_send, z_recv, y_send, y_recv,
    w_send, w_recv, m_send, m_recv, mt_send, mt_recv,
):
    s, t, z, y, x, c = coords()
    rows = tok.shape[0]
    depth = w.shape[2]
    x_peer = (s, (1 - x) * 2 + c)
    core_peer = (s, x * 2 + (1 - c))
    diagonal = (s, (1 - x) * 2 + (1 - c))
    y_peer = (z * 2 + (1 - y), t)
    seq_peers = [(lax.rem(s + k, 8), t) for k in range(1, 8)]
    enter(seq_peers + [x_peer, core_peer, diagonal])

    piece = rows // PIECES

    def tok_at(block, p):
        return tok_all.at[pl.ds(pl.multiple_of(block * rows + p * piece, piece), piece)]

    def mine(p):
        return tok.at[pl.ds(p * piece, piece)]

    def w_at(owner, m, h):
        return w_all.at[m, h, pl.ds(pl.multiple_of(owner * depth, depth), depth)]

    chunks = [(m, h) for m in range(w.shape[0]) for h in range(w.shape[1])]

    def up(o, p, src):
        return remote(src, tok_at(o * 2 + y, p), up_send.at[o, p], z_recv.at[o, p], (s + 2, t))

    def down(o, p, src):
        return remote(src, tok_at(o * 2 + y, p), dn_send.at[o, p], z_recv.at[o, p], (s - 2, t))

    def across(o, p, src):
        return remote(src, tok_at(o * 2 + y, p), y_send.at[o, p], y_recv.at[o, p], y_peer)

    def w_copy(kind, k, src, owner, peer):
        m, h = chunks[k]
        return remote(src, w_at(owner, m, h), w_send.at[kind, k], w_recv.at[kind, k], peer)

    for p in range(PIECES):
        @pl.when(z < 3)
        def _():
            up(z, p, mine(p)).start()

        @pl.when(z > 0)
        def _():
            down(z, p, mine(p)).start()

        across(z, p, mine(p)).start()
    for k, (m, h) in enumerate(chunks):
        w_copy(0, k, w.at[m, h], t, x_peer).start()
    meta_copies = [
        remote(meta, meta_all.at[t, s], m_send.at[k], m_recv.at[k], peer)
        for k, peer in enumerate(seq_peers)
    ]
    for copy in meta_copies:
        copy.start()
    for k, (m, h) in enumerate(chunks):
        w_copy(1, k, w.at[m, h], t, core_peer).start()
    def near_up():
        return remote(w_out, near_low, n_send.at[0], n_recv.at[0], (s + 2, t))

    def near_down():
        return remote(w_out, near_high, n_send.at[1], n_recv.at[1], (s - 2, t))

    @pl.when(z < 3)
    def _():
        near_up().start()

    @pl.when(z > 0)
    def _():
        near_down().start()

    own_rows = tok_all.at[pl.ds(pl.multiple_of(s * rows, rows), rows)]
    staged = [pltpu.make_async_copy(tok, tok_buf, local_sem.at[0])]
    own = [
        pltpu.make_async_copy(tok_buf, own_rows, local_sem.at[1]),
        pltpu.make_async_copy(meta, meta_all.at[t, s], local_sem.at[2]),
    ]
    for k, (m, h) in enumerate(chunks):
        staged.append(pltpu.make_async_copy(w.at[m, h], w_buf.at[k], local_sem.at[3 + 2 * k]))
        own.append(pltpu.make_async_copy(w_buf.at[k], w_at(t, m, h), local_sem.at[4 + 2 * k]))
    for copy in staged:
        copy.start()
    for copy in staged:
        copy.wait()
    for copy in own:
        copy.start()

    def pass_weights(k):
        m, h = chunks[k]
        w_copy(0, k, w.at[m, h], t, x_peer).wait_recv()
        w_copy(2, k, w_at(x_peer[1], m, h), x_peer[1], core_peer).start()

    n_chunks = len(chunks)
    for d in range(1, 4):
        if d - 1 < n_chunks:
            pass_weights(d - 1)
        low, high = z - d, z + d
        for p in range(PIECES):
            @pl.when(low >= 0)
            def _():
                src = tok_at(low * 2 + y, p)
                up(low, p, src).wait_recv()

                @pl.when(z < 3)
                def _():
                    up(low, p, src).start()

                across(low, p, src).start()

            @pl.when(high <= 3)
            def _():
                src = tok_at(high * 2 + y, p)
                down(high, p, src).wait_recv()

                @pl.when(z > 0)
                def _():
                    down(high, p, src).start()

                across(high, p, src).start()

    for k in range(3, n_chunks):
        pass_weights(k)
    for copy in own:
        copy.wait()
    for copy in meta_copies:
        copy.wait()
    tower_meta = [
        remote(meta_all.at[t], meta_all.at[t], mt_send.at[k], mt_recv.at[k], peer)
        for k, peer in enumerate((x_peer, core_peer, diagonal))
    ]
    for copy in tower_meta:
        copy.start()
    for o in range(4):
        for p in range(PIECES):
            across(o, p, mine(p)).wait()

            @pl.when((z < 3) & (o <= z))
            def _():
                up(o, p, mine(p)).wait_send()

            @pl.when((z > 0) & (o >= z))
            def _():
                down(o, p, mine(p)).wait_send()

    for k, (m, h) in enumerate(chunks):
        w_copy(0, k, w.at[m, h], t, x_peer).wait_send()
        w_copy(1, k, w.at[m, h], t, core_peer).wait()
        w_copy(2, k, w.at[m, h], t, core_peer).wait()
    for copy in tower_meta:
        copy.wait()

    @pl.when(z < 3)
    def _():
        near_up().wait_send()
        near_down().wait_recv()

    @pl.when(z > 0)
    def _():
        near_down().wait_send()
        near_up().wait_recv()


def gather_all(tok, meta, w, w_out):
    dma = pltpu.SemaphoreType.DMA
    hbm = pl.BlockSpec(memory_space=pl.ANY)
    heads = w.shape[1]
    return pl.pallas_call(
        gather_kernel,
        out_shape=(
            jax.ShapeDtypeStruct((tok.shape[0] * 8, tok.shape[1]), tok.dtype),
            jax.ShapeDtypeStruct((4, 8) + meta.shape, meta.dtype),
            jax.ShapeDtypeStruct((2, heads, w.shape[2] * 4, w.shape[3]), w.dtype),
            jax.ShapeDtypeStruct(w_out.shape, w_out.dtype),
            jax.ShapeDtypeStruct(w_out.shape, w_out.dtype),
        ),
        in_specs=[hbm] * 4,
        out_specs=(hbm,) * 5,
        scratch_shapes=[
            pltpu.VMEM((2 * heads,) + w.shape[2:], w.dtype), pltpu.VMEM(tok.shape, tok.dtype),
            dma((3 + 4 * heads,)), dma((2,)), dma((2,)), dma((4, PIECES)), dma((4, PIECES)), dma((4, PIECES)),
            dma((4, PIECES)), dma((4, PIECES)),
            dma((3, 2 * heads)), dma((3, 2 * heads)), dma((7,)), dma((7,)), dma((3,)), dma((3,)),
        ],
        compiler_params=pltpu.CompilerParams(
            collective_id=0, has_side_effects=True, vmem_limit_bytes=56 << 20
        ),
        cost_estimate=pl.CostEstimate(flops=0, bytes_accessed=42 << 20, transcendentals=0),
    )(tok, meta, w, w_out)


def out_kernel(
    ho, mask, w0, w1, w2, w3, out, got, lhs, keep, sent, arrived, ready,
    z_send, z_recv, g_send, g_recv, y_send, y_recv, o_send, o_recv,
):
    s, t, z, y, x, c = coords()
    rows = ho.shape[0] // 4
    half = rows // 2
    width = ho.shape[1]
    cols = w0.shape[1]
    below = jnp.where(z == 0, 1, z - 1)
    across = lax.rem(z + 2, 4)
    groups = [(z, w0), (below, w1), (across, w2), (6 - z - below - across, w3)]
    order = [t, x * 2 + (1 - c), (1 - x) * 2 + c, (1 - x) * 2 + (1 - c)]
    x_peer, core_peer = (s, order[2]), (s, order[1])
    y_peer = (z * 2 + (1 - y), t)
    z_peers = [(lax.rem(s + 2 * k, 8), t) for k in range(1, 4)]
    enter(z_peers + [(s, o) for o in order[1:]] + [y_peer])

    def rows_of(block, n):
        return pl.ds(pl.multiple_of(block * n, n), n)

    z_copies = [
        remote(
            ho.at[rows_of(lax.rem(z + k, 4), rows)], got.at[t, z],
            z_send.at[k - 1], z_recv.at[k - 1], z_peers[k - 1],
        )
        for k in range(1, 4)
    ]
    for copy in z_copies:
        copy.start()
    got[t, z] = ho[rows_of(z, rows)]
    origins = [z] + [lax.rem(z + k, 4) for k in (3, 1, 2)]

    def g_copy(kind, i):
        block = got.at[order[2] if kind == 2 else t, origins[i]]
        peer = x_peer if kind == 0 else core_peer
        return remote(block, block, g_send.at[kind, i], g_recv.at[kind, i], peer)

    for i, k in enumerate((0, 1, 3, 2)):
        if k:
            z_copies[k - 1].wait_recv()
        g_copy(0, i).start()
        g_copy(1, i).start()

    def project(j):
        owner = order[j]
        for g in range(4):
            block = got[owner, groups[g][0]]
            m = mask[owner]
            for h in range(width // 128):
                part = block[:, h * 128:(h + 1) * 128]
                image = part * m
                lhs[g, :, h * 128:(h + 1) * 128] = part - image
                lhs[g, :, width + h * 128:width + (h + 1) * 128] = image

        for away in (1, 0):
            side = (1 - y) if away else y

            @pl.loop(0, cols // 256)
            def _(tile):
                at = rows_of(tile, 256)
                total = None
                for g in range(4):
                    part = jnp.dot(
                        lhs[g, rows_of(side, half), :], groups[g][1][:, at],
                        preferred_element_type=jnp.float32,
                    ).astype(jnp.bfloat16).astype(jnp.float32)
                    total = part if total is None else total + part
                if away:
                    sent[j, :, at] = total.astype(jnp.bfloat16)
                else:
                    keep[j, :, at] = total

            if away:
                y_copies[j].start()

    y_copies = [
        remote(sent.at[j], arrived.at[j], y_send.at[j], y_recv.at[j], y_peer) for j in range(4)
    ]
    my_cols = rows_of(t, cols)
    o_copies = [
        remote(ready.at[j], out.at[:, my_cols], o_send.at[j - 1], o_recv.at[j - 1], (s, order[j]))
        for j in range(1, 4)
    ]

    def finish(j):
        y_copies[j].wait_recv()
        total = (keep[j] + arrived[j].astype(jnp.float32)).astype(jnp.bfloat16)
        if j == 0:
            out[:, my_cols] = total
        else:
            ready[j] = total
            o_copies[j - 1].start()

    for i in range(4):
        g_copy(1, i).wait_recv()
    project(1)
    for i in range(4):
        g_copy(0, i).wait_recv()
        g_copy(2, i).start()
    project(2)
    for i in range(4):
        g_copy(2, i).wait_recv()
    project(3)
    finish(1)
    project(0)
    finish(2)
    finish(3)
    finish(0)
    for copy in z_copies + y_copies:
        copy.wait_send()
    for kind in range(3):
        for i in range(4):
            g_copy(kind, i).wait_send()
    for copy in o_copies:
        copy.wait()


def out_project(ho, mask, ws):
    dma = pltpu.SemaphoreType.DMA
    vmem = pl.BlockSpec(memory_space=pltpu.VMEM)
    rows, cols, width = ho.shape[0] // 4, ws[0].shape[1], ho.shape[1]
    return pl.pallas_call(
        out_kernel,
        out_shape=jax.ShapeDtypeStruct((rows // 2, cols * 4), jnp.bfloat16),
        in_specs=[vmem] * 6,
        out_specs=vmem,
        scratch_shapes=[
            pltpu.VMEM((4, 4, rows, width), jnp.bfloat16),
            pltpu.VMEM((4, rows, 2 * width), jnp.bfloat16),
            pltpu.VMEM((4, rows // 2, cols), jnp.float32),
            pltpu.VMEM((4, rows // 2, cols), jnp.bfloat16),
            pltpu.VMEM((4, rows // 2, cols), jnp.bfloat16),
            pltpu.VMEM((4, rows // 2, cols), jnp.bfloat16),
            dma((3,)), dma((3,)), dma((3, 4)), dma((3, 4)), dma((4,)), dma((4,)), dma((3,)), dma((3,)),
        ],
        compiler_params=pltpu.CompilerParams(
            collective_id=1, has_side_effects=True, vmem_limit_bytes=40 << 20
        ),
        cost_estimate=pl.CostEstimate(
            flops=4 * 1024 * 1024 * 1024, bytes_accessed=8 << 20, transcendentals=0
        ),
    )(ho, mask, *ws)


def fast_local(inputs, modality, segment, w_qkv, w_out):
    heads, head_size = w_qkv.shape[1], w_out.shape[2]
    score_scale = 1.0 / math.sqrt(head_size)
    meta = jnp.concatenate([modality, segment, jnp.zeros((6, modality.shape[1]), jnp.int32)], axis=0)
    tok_all, meta_all, weights, near_low, near_high = gather_all(inputs[0], meta, w_qkv, w_out)
    s, t, z, y, x, c = coords()
    up_pairs = [(a * 2 + b, (a + 1) * 2 + b) for a in (1, 2) for b in (0, 1)]
    down_pairs = [(a * 2 + b, (a - 1) * 2 + b) for a in (1, 2) for b in (0, 1)]
    end_pairs = [(2 + b, b) for b in (0, 1)] + [(4 + b, 6 + b) for b in (0, 1)]
    from_low = lax.ppermute(near_low, "seq", up_pairs)
    from_high = lax.ppermute(near_high, "seq", down_pairs)
    far = jnp.where(z >= 2, from_low, from_high)
    last = lax.ppermute(far, "seq", end_pairs)
    blocks = [
        w_out,
        jnp.where(z == 0, near_high, near_low),
        far,
        jnp.where((z == 0) | (z == 3), last, near_high),
    ]
    columns = [b.reshape(2 * heads * head_size, w_out.shape[3]) for b in blocks]
    mine = lax.dynamic_index_in_dim(meta_all, t, 0, keepdims=False)
    modal_all = mine[:, 0].reshape(-1)
    doc_all = mine[:, 1].reshape(-1)
    text_part = qkv_product(tok_all, weights[0])
    image_part = qkv_product(tok_all, weights[1])
    projected = jnp.where(modal_all[:, None, None] == 1, image_part, text_part).astype(jnp.bfloat16)
    head_list = []
    for head_idx in range(heads):
        queries = projected[:, head_idx, :head_size]
        keys_all = projected[:, head_idx, head_size : 2 * head_size]
        values_all = projected[:, head_idx, 2 * head_size :]
        head_list.append(dense_attend(queries, keys_all, values_all, doc_all, score_scale))
    ho = jnp.concatenate(head_list, axis=1)
    block = lax.dynamic_slice_in_dim(meta_all[:, :, 0], z * 2, 2, 1)
    block = (block.reshape(4, -1, 1) == 1).astype(jnp.bfloat16)
    mask = jnp.broadcast_to(block, (4, block.shape[1], 128))
    return out_project(ho, mask, columns)[None]


def solution(mesh):
    small = mesh.shape["seq"] == 8 and mesh.shape["tower"] == 4
    return jax.shard_map(
        fast_local if small else local,
        mesh=mesh,
        in_specs=(
            P("tower", "seq", None),
            P("tower", "seq"),
            P("tower", "seq"),
            P(None, "seq", "tower", None),
            P(None, "seq", None, "tower"),
        ),
        out_specs=P("tower", "seq", None),
        check_vma=False,
    )
```
